32 devices in a mesh: shots: 2 (over y), bx: 4 (over z), by: 2 (over x), bz: 2 (over core).
Axes of the slice: x: 2, y: 2, z: 4, core: 2. Of those that a mesh axis runs over, the one named last changes fastest.
Arguments:
- weights: bfloat16 [16384, 2, 256], P(('shots', 'bx', 'by', 'bz')), parts along dimension 0, may hold values from -6 to 6
- interp: bfloat16 [2, 2, 256, 256], replicated, may hold values from -0.25 to 0.25
- slowness: float32 [2, 2, 256], replicated, may hold values from -0.05 to 0.05
- box_coord: int32 [2, 8192], P(None, ('bx', 'by', 'bz')), may hold values from 0 to 127
Outputs:
- result: bfloat16 [16384, 2, 256], P(('shots', 'bx', 'by', 'bz')), parts along dimension 0
The draws below stay inside these ranges and needn't reach their ends.
There are 2 independent parts, one for each index of `shots`. The reference program is written for one: setup_inputs(seed, part) draws one part's arguments, and reference() takes and returns one part's arrays. A program takes and returns all parts, laid end to end along the dimension named above; an argument that names none is the same for every part. Nothing has to cross between parts.
All inputs are finite; a program needn't handle non-finite values.
Results may differ from the reference program's by a relative error of at most 0.022.
Values may be sent and summed in bfloat16 or wider, within the bound.
A program may use at most 64 MiB of HBM per device.

```python
import jax
import jax.numpy as jnp

RANK = 256
SLOTS_DEV = 512
LOCAL = 4
BOXES = 128
SLOTS = 8192
N_BX = 4
N_BY = 2
N_BZ = 2


def touch_ends(entries, own_key, least, largest):
    dims = entries.shape
    index_at = [jax.random.randint(jax.random.fold_in(own_key, axis), (), 0, dims[axis]) for axis in range(len(dims))]
    entries = entries.at[tuple(index_at)].set(least)
    longest = dims.index(max(dims))
    index_at[longest] = (index_at[longest] + 1) % dims[longest]
    return entries.at[tuple(index_at)].set(largest)


def shard_levels(rng, extent, shards, low, top_value):
    gain = 1.0
    for position, shards_of in shards:
        heights = jax.random.uniform(jax.random.fold_in(jax.random.fold_in(rng, 6), position), (shards_of,), jnp.float32, low / len(shards), top_value / len(shards))
        gain = gain * jnp.repeat(jnp.exp(heights), extent[position] // shards_of).reshape((-1,) + (1,) * (len(extent) - 1 - position))
    return gain


def normal_values(own_key, shape, deviation, limit, cuts=(), dtype=jnp.bfloat16):
    entries = jax.random.normal(own_key, shape, jnp.float32) * deviation
    if len(cuts) > 0:
        entries = shard_levels(own_key, shape, cuts, -0.22, 0.18) * entries
    return jnp.clip(entries, min=-limit, max=limit).astype(dtype)


def setup_inputs(seed: int = 0, part: int = 0) -> dict:
    key_list = jax.random.split(jax.random.key(seed), 5)
    part_keys = jax.random.split(jax.random.fold_in(key_list[4], part), 5)
    return {
        "weights": normal_values(part_keys[0], (SLOTS, 2, RANK), 1.0, 6.0, ((0, 16),)),
        "interp": normal_values(key_list[1], (2, 2, RANK, RANK), (2 * RANK) ** -0.5, 0.25),
        "slowness": jnp.clip(jax.random.uniform(key_list[2], (2, 2, RANK), jnp.float32, -0.05, 0.05), -0.05, 0.05),
        "box_coord": touch_ends(jax.random.randint(key_list[3], (2, SLOTS), 0, BOXES), jax.random.fold_in(key_list[3], 1), 0, BOXES - 1).astype(jnp.int32),
    }


def apply_matrix(block, matrix):
    block_shape = block.shape
    product = jnp.dot(block.reshape(-1, block_shape[-1]), matrix, preferred_element_type=jnp.float32)
    return product.reshape(block_shape)


def rotate_phase(summed, cosine, sine):
    real_part = summed[..., 0, :]
    imag_part = summed[..., 1, :]
    return jnp.stack([cosine * real_part - sine * imag_part, sine * real_part + cosine * imag_part], axis=-2).astype(jnp.bfloat16)


def level_step(grouped, interp, cos_group, sin_group):
    first_child = grouped[:, 0]
    second_child = grouped[:, 1]
    results = []
    for target in range(2):
        summed = apply_matrix(first_child, interp[target, 0]) + apply_matrix(second_child, interp[target, 1])
        results.append(rotate_phase(summed, cos_group[:, target], sin_group[:, target]))
    return jnp.stack(results, axis=1)


def reference(weights, interp, slowness, box_coord):
    groups = N_BX * N_BY * N_BZ
    per_dev = SLOTS_DEV
    coords = box_coord.astype(jnp.float32)
    dist_angle = coords[0][:, None] * slowness[0, 0][None, :] + coords[1][:, None] * slowness[0, 1][None, :]
    local_angle = coords[0][:, None] * slowness[1, 0][None, :] + coords[1][:, None] * slowness[1, 1][None, :]
    dist_cos = jnp.cos(dist_angle)
    dist_sin = jnp.sin(dist_angle)
    local_cos = jnp.cos(local_angle)
    local_sin = jnp.sin(local_angle)
    current = weights
    bit_count = groups.bit_length() - 1
    for bit_num in range(bit_count):
        spread = 2 ** bit_num
        outer = groups // (2 * spread)
        grouped = current.reshape(outer, 2, spread * per_dev, 2, RANK)
        cos_group = dist_cos.reshape(outer, 2, spread * per_dev, RANK)
        sin_group = dist_sin.reshape(outer, 2, spread * per_dev, RANK)
        current = level_step(grouped, interp, cos_group, sin_group).reshape(-1, 2, RANK)
    for local_num in range(LOCAL):
        span_len = per_dev >> (local_num + 1)
        grouped = current.reshape(-1, 2, span_len, 2, RANK)
        cos_group = local_cos.reshape(-1, 2, span_len, RANK)
        sin_group = local_sin.reshape(-1, 2, span_len, RANK)
        current = level_step(grouped, interp, cos_group, sin_group).reshape(-1, 2, RANK)
    return current
```

```python
import functools
import math

import jax
import jax.numpy as jnp
from jax import lax
from jax.experimental import pallas as pl
from jax.experimental.pallas import tpu as pltpu
from jax.sharding import PartitionSpec as P

LOCAL = 4
MESH = pl.DeviceIdType.MESH
F32 = jnp.float32
BF16 = jnp.bfloat16
SUB = 8

SIN_TERMS = [(-1) ** i * math.pi ** (2 * i + 1) / math.factorial(2 * i + 1) for i in range(6)]
COS_TERMS = [(-1) ** i * math.pi ** (2 * i) / math.factorial(2 * i) for i in range(6)]


def horner(terms, square):
    total = jnp.full_like(square, terms[-1])
    for term in terms[-2::-1]:
        total = total * square + term
    return total


def cos_sin(angle):
    turns = angle * (1.0 / (2.0 * math.pi))
    frac = turns - jnp.round(turns)
    square = frac * frac
    half_sin = frac * horner(SIN_TERMS, square)
    half_cos = horner(COS_TERMS, square)
    return 1.0 - 2.0 * half_sin * half_sin, 2.0 * half_sin * half_cos


def shuffle_matrix(rows, inverse):
    worked = lax.broadcasted_iota(jnp.int32, (rows, rows), 1 if inverse else 0)
    stored = lax.broadcasted_iota(jnp.int32, (rows, rows), 0 if inverse else 1)
    source = (
        (worked // 32) * 32
        + (worked % 8) * 4
        + ((worked // 16) % 2) * 2
        + (worked // 8) % 2
    )
    return jnp.where(stored == source, 1.0, 0.0).astype(BF16)


def rotate(summed, cosine, sine):
    real_part, imag_part = summed[:, 0], summed[:, 1]
    return jnp.stack(
        [cosine * real_part - sine * imag_part, sine * real_part + cosine * imag_part], axis=1
    )


def dot(a, b):
    return jnp.dot(a, b, preferred_element_type=F32)


def kernel(
    levels, w_ref, interp_ref, slow_ref, coord_ref, out_ref,
    cur, got, dcos, dsin, lcos, lsin, padded, columns, send_sem, recv_sem,
):
    depth = len(levels)
    high, nk = w_ref.shape[0], w_ref.shape[1]
    half = high // 2
    chunks = 2 * nk
    rows = half * 2 * SUB
    rank = interp_ref.shape[-1]

    upper, partner = [], []
    for axis, bit in levels:
        me = lax.axis_index(axis)
        up = (me // (1 << bit)) % 2
        upper.append(up)
        partner.append({axis: me + (1 << bit) * (1 - 2 * up)})

    barrier = pltpu.get_barrier_semaphore()
    for device in partner:
        pl.semaphore_signal(barrier, inc=1, device_id=device, device_id_type=MESH)
    pl.semaphore_wait(barrier, depth)

    def copy(level, m):
        return pltpu.make_async_remote_copy(
            src_ref=cur.at[level, m],
            dst_ref=got.at[level, m],
            send_sem=send_sem.at[level, m],
            recv_sem=recv_sem.at[level, m],
            device_id=partner[level],
            device_id_type=MESH,
        )

    spread = shuffle_matrix(half * 32, False)

    def load(m):
        k, top = m // 2, (m % 2) * half
        stored = w_ref[top : top + half, k].reshape(half * 32, 128)
        moved = dot(spread, stored).reshape(half, 2, 2 * SUB, 128)
        block = jnp.concatenate([moved[:, 0], moved[:, 1]], axis=-1)
        cur[0, m] = block.reshape(rows, rank).astype(BF16)
        copy(0, m).start()

    def angles(m, table, cos_ref, sin_ref):
        k, top = m // 2, (m % 2) * half
        column = columns[top : top + half, k].reshape(half * SUB, 8)
        angle = column[:, 0:1] * slow_ref[table, 0:1] + column[:, 1:2] * slow_ref[table, 1:2]
        cosine, sine = cos_sin(angle)
        cos_ref[m] = cosine.reshape(half, SUB, rank)
        sin_ref[m] = sine.reshape(half, SUB, rank)

    def device_step(level, m):
        up = upper[level]
        mine = dot(cur[level, m], interp_ref[up, up])
        copy(level, m).wait_recv()
        summed = mine + dot(got[level, m], interp_ref[up, 1 - up])
        turned = rotate(summed.reshape(half, 2, SUB, rank), dcos[m], dsin[m])
        cur[level + 1, m] = turned.reshape(rows, rank).astype(BF16)
        if level + 1 < depth:
            copy(level + 1, m).start()

    gather = shuffle_matrix(half * 32, True)

    def local_steps(k):
        block = cur[depth, 2 * k : 2 * k + 2].reshape(high, 2 * SUB, rank)
        cosine = lcos[2 * k : 2 * k + 2].reshape(high, SUB, rank)
        sine = lsin[2 * k : 2 * k + 2].reshape(high, SUB, rank)
        for num in range(LOCAL):
            outer, inner = 1 << num, high >> (num + 1)
            pair = block.reshape(outer, 2, inner, 2 * SUB, rank)
            first = pair[:, 0].reshape(-1, rank)
            second = pair[:, 1].reshape(-1, rank)
            cos_pair = cosine.reshape(outer, 2, inner, SUB, rank)
            sin_pair = sine.reshape(outer, 2, inner, SUB, rank)
            results = []
            for target in range(2):
                summed = dot(first, interp_ref[target, 0]) + dot(second, interp_ref[target, 1])
                turned = rotate(
                    summed.reshape(outer * inner, 2, SUB, rank),
                    cos_pair[:, target].reshape(-1, SUB, rank),
                    sin_pair[:, target].reshape(-1, SUB, rank),
                )
                results.append(turned.astype(BF16).reshape(outer, inner, 2 * SUB, rank))
            block = jnp.stack(results, axis=1).reshape(high, 2 * SUB, rank)
        for part in range(2):
            top = part * half
            piece = block[top : top + half]
            worked = jnp.stack([piece[..., :128], piece[..., 128:]], axis=1)
            stored = dot(gather, worked.reshape(half * 32, 128))
            out_ref[top : top + half, k] = stored.reshape(half, 32, 128).astype(BF16)

    for m in range(chunks):
        load(m)
    padded[...] = jnp.zeros_like(padded)
    padded[0:2] = coord_ref[...].astype(F32)
    columns[...] = padded[...].T.reshape(columns.shape)

    tasks = []
    for level in range(depth):
        rate = 0.2 if level == 0 else 2.6 if level == depth - 1 else 1.4
        for m in range(chunks):
            tasks.append((2.5 * level + rate * m, 1, "device", level, m))
    for m in range(chunks):
        tasks.append((0.2 * m, 0, "dist", 0, m))
        tasks.append((3.0 + 1.2 * m, 2, "local", 0, m))
    for k in range(nk):
        tasks.append((2.5 * (depth - 1) + 2.6 * (2 * k + 1), 3, "steps", 0, k))
    for _, _, kind, level, m in sorted(tasks):
        if kind == "device":
            device_step(level, m)
        elif kind == "dist":
            angles(m, 0, dcos, dsin)
        elif kind == "local":
            angles(m, 1, lcos, lsin)
        else:
            local_steps(m)

    for level in range(depth):
        for m in range(chunks):
            copy(level, m).wait_send()


def solution(mesh):
    levels = []
    for axis in ("bz", "by", "bx"):
        levels += [(axis, bit) for bit in range(mesh.shape[axis].bit_length() - 1)]

    def local(weights, interp, slowness, box_coord):
        per_dev, _, rank = weights.shape
        high = 1 << LOCAL
        nk = per_dev // (high * SUB)
        half = high // 2
        depth, chunks, rows = len(levels), 2 * nk, half * 2 * SUB
        stored = weights.reshape(per_dev, 2, 2, 128).transpose(0, 2, 1, 3)
        stored = stored.reshape(high, nk, 4 * SUB, 128)
        table = pltpu.VMEM((chunks, half, SUB, rank), F32)
        result = pl.pallas_call(
            functools.partial(kernel, levels),
            out_shape=jax.ShapeDtypeStruct(stored.shape, BF16),
            in_specs=[pl.BlockSpec(memory_space=pltpu.VMEM)] * 4,
            out_specs=pl.BlockSpec(memory_space=pltpu.VMEM),
            scratch_shapes=[
                pltpu.VMEM((depth + 1, chunks, rows, rank), BF16),
                pltpu.VMEM((depth, chunks, rows, rank), BF16),
                table, table, table, table,
                pltpu.VMEM((8, per_dev), F32),
                pltpu.VMEM((high, nk, SUB, 8), F32),
                pltpu.SemaphoreType.DMA((depth, chunks)),
                pltpu.SemaphoreType.DMA((depth, chunks)),
            ],
            compiler_params=pltpu.CompilerParams(
                collective_id=0, has_side_effects=True, vmem_limit_bytes=48 * 1024 * 1024
            ),
        )(stored, interp, slowness, box_coord)
        result = result.reshape(per_dev, 2, 2, 128).transpose(0, 2, 1, 3)
        return result.reshape(per_dev, 2, rank)

    return jax.shard_map(
        local,
        mesh=mesh,
        in_specs=(P(("shots", "bx", "by", "bz"), None, None), P(), P(), P(None, ("bx", "by", "bz"))),
        out_specs=P(("shots", "bx", "by", "bz"), None, None),
        check_vma=False,
    )
```

```python
import functools
import math

import jax
import jax.numpy as jnp
from jax import lax
from jax.experimental import pallas as pl
from jax.experimental.pallas import tpu as pltpu
from jax.sharding import PartitionSpec as P

LOCAL = 4
MESH = pl.DeviceIdType.MESH
F32 = jnp.float32
BF16 = jnp.bfloat16
SUB = 8

SIN_TERMS = [(-1) ** i * math.pi ** (2 * i + 1) / math.factorial(2 * i + 1) for i in range(6)]
COS_TERMS = [(-1) ** i * math.pi ** (2 * i) / math.factorial(2 * i) for i in range(6)]


def horner(terms, square):
    total = jnp.full_like(square, terms[-1])
    for term in terms[-2::-1]:
        total = total * square + term
    return total


def cos_sin(angle):
    turns = angle * (1.0 / (2.0 * math.pi))
    frac = turns - jnp.round(turns)
    square = frac * frac
    half_sin = frac * horner(SIN_TERMS, square)
    half_cos = horner(COS_TERMS, square)
    return 1.0 - 2.0 * half_sin * half_sin, 2.0 * half_sin * half_cos


def shuffle_matrix(rows, inverse):
    worked = lax.broadcasted_iota(jnp.int32, (rows, rows), 1 if inverse else 0)
    stored = lax.broadcasted_iota(jnp.int32, (rows, rows), 0 if inverse else 1)
    source = (
        (worked // 32) * 32
        + (worked % 8) * 4
        + ((worked // 16) % 2) * 2
        + (worked // 8) % 2
    )
    return jnp.where(stored == source, 1.0, 0.0).astype(BF16)


def rotate(summed, cosine, sine):
    real_part, imag_part = summed[:, 0], summed[:, 1]
    return jnp.stack(
        [cosine * real_part - sine * imag_part, sine * real_part + cosine * imag_part], axis=1
    )


def dot(a, b):
    return jnp.dot(a, b, preferred_element_type=F32)


def kernel(
    levels, w_hbm, interp_hbm, slow_hbm, coord_hbm, out_ref,
    w_ref, interp_ref, slow_ref, coord_ref, raw, done, cur, got,
    dcos, dsin, lcos, lsin, padded, columns,
    in_sem, send_sem, recv_sem, raw_send, raw_recv, coord_send, coord_recv, done_send, done_recv,
):
    depth = len(levels)
    top = depth - 1
    high, nk = w_ref.shape[0], w_ref.shape[1]
    half = high // 2
    rows = half * 2 * SUB
    rank = interp_ref.shape[-1]
    nd, nf = nk // 2, nk // 4
    direct, owned = 2 * nd, 2 * nf
    items = direct + 2 * owned

    upper, partner = [], []
    for axis, bit in levels:
        me = lax.axis_index(axis)
        up = (me // (1 << bit)) % 2
        upper.append(up)
        partner.append({axis: me + (1 << bit) * (1 - 2 * up)})
    side = upper[top]

    def group_of(item):
        if item < direct:
            return item // 2
        return nd + side * nf + ((item - direct) % owned) // 2

    def fetch(src, dst, n):
        return pltpu.make_async_copy(src, dst, in_sem.at[n])

    fetches = [
        fetch(w_hbm.at[:, group_of(2 * n)], w_ref.at[:, group_of(2 * n)], n) for n in range(nd + nf)
    ]
    fetch_coord = fetch(coord_hbm, coord_ref.at[0], nd + nf)
    fetch_slow = fetch(slow_hbm, slow_ref, nd + nf + 1)
    fetch_interp = fetch(interp_hbm, interp_ref, nd + nf + 2)
    for one in [fetches[0], fetch_coord, fetch_slow, fetch_interp] + fetches[1:]:
        one.start()

    barrier = pltpu.get_barrier_semaphore()
    for device in partner:
        pl.semaphore_signal(barrier, inc=1, device_id=device, device_id_type=MESH)
    pl.semaphore_wait(barrier, depth)

    def remote(src, dst, sent, received, level):
        return pltpu.make_async_remote_copy(
            src_ref=src, dst_ref=dst, send_sem=sent, recv_sem=received,
            device_id=partner[level], device_id_type=MESH,
        )

    def copy(level, item):
        return remote(
            cur.at[level, item], got.at[level, item],
            send_sem.at[level, item], recv_sem.at[level, item], level,
        )

    def copy_raw(n):
        group = nd + (1 - side) * nf + n // 2
        src = w_hbm.at[pl.ds((n % 2) * half, half), group]
        return remote(src, raw.at[n], raw_send.at[n], raw_recv.at[n], top)

    copy_coord = remote(coord_hbm, coord_ref.at[1], coord_send, coord_recv, top)

    def copy_done(n, owner):
        dst = out_ref.at[pl.ds((n % 2) * half, half), nd + owner * nf + n // 2]
        return remote(done.at[n], dst, done_send.at[n], done_recv.at[n], top)

    copy_coord.start()
    for n in range(owned):
        copy_raw(n).start()

    spread = shuffle_matrix(half * 32, False)
    gather = shuffle_matrix(half * 32, True)

    def load(item):
        if item < direct + owned:
            if item % 2 == 0:
                fetches[item // 2].wait()
            first = (item % 2) * half
            stored = w_ref[first : first + half, group_of(item)]
        else:
            n = item - direct - owned
            copy_raw(n).wait_recv()
            stored = raw[n]
        moved = dot(spread, stored.reshape(half * 32, 128)).reshape(half, 2, 2 * SUB, 128)
        block = jnp.concatenate([moved[:, 0], moved[:, 1]], axis=-1)
        cur[0, item] = block.reshape(rows, rank).astype(BF16)
        copy(0, item).start()

    def place(which):
        if which == 0:
            fetch_coord.wait()
            fetch_slow.wait()
            padded[...] = jnp.zeros_like(padded)
        else:
            copy_coord.wait_recv()
        padded[0:2] = coord_ref[which].astype(F32)
        columns[which] = padded[...].T.reshape(columns.shape[1:])

    def angles(item, table, cos_ref, sin_ref):
        first = (item % 2) * half
        which = 1 if item >= direct + owned else 0
        column = columns[which, first : first + half, group_of(item)].reshape(half * SUB, 8)
        angle = column[:, 0:1] * slow_ref[table, 0:1] + column[:, 1:2] * slow_ref[table, 1:2]
        cosine, sine = cos_sin(angle)
        cos_ref[item] = cosine.reshape(half, SUB, rank)
        sin_ref[item] = sine.reshape(half, SUB, rank)

    def device_step(level, item):
        up = upper[level]
        mine = dot(cur[level, item], interp_ref[up, up])
        copy(level, item).wait_recv()
        summed = mine + dot(got[level, item], interp_ref[up, 1 - up])
        turned = rotate(summed.reshape(half, 2, SUB, rank), dcos[item], dsin[item])
        cur[level + 1, item] = turned.reshape(rows, rank).astype(BF16)
        if level + 1 < top or (level + 1 == top and item < direct):
            copy(level + 1, item).start()

    def local_steps(block, item):
        cosine = lcos[item : item + 2].reshape(high, SUB, rank)
        sine = lsin[item : item + 2].reshape(high, SUB, rank)
        for num in range(LOCAL):
            outer, inner = 1 << num, high >> (num + 1)
            pair = block.reshape(outer, 2, inner, 2 * SUB, rank)
            first = pair[:, 0].reshape(-1, rank)
            second = pair[:, 1].reshape(-1, rank)
            cos_pair = cosine.reshape(outer, 2, inner, SUB, rank)
            sin_pair = sine.reshape(outer, 2, inner, SUB, rank)
            results = []
            for target in range(2):
                summed = dot(first, interp_ref[target, 0]) + dot(second, interp_ref[target, 1])
                turned = rotate(
                    summed.reshape(outer * inner, 2, SUB, rank),
                    cos_pair[:, target].reshape(-1, SUB, rank),
                    sin_pair[:, target].reshape(-1, SUB, rank),
                )
                results.append(turned.astype(BF16).reshape(outer, inner, 2 * SUB, rank))
            block = jnp.stack(results, axis=1).reshape(high, 2 * SUB, rank)
        return block

    def as_stored(block, part):
        piece = block[part * half : (part + 1) * half]
        worked = jnp.stack([piece[..., :128], piece[..., 128:]], axis=1)
        stored = dot(gather, worked.reshape(half * 32, 128))
        return stored.reshape(half, 32, 128).astype(BF16)

    def finish(block, item):
        block = local_steps(block, item)
        for part in range(2):
            out_ref[part * half : (part + 1) * half, group_of(item)] = as_stored(block, part)

    def direct_end(k):
        block = cur[depth, 2 * k : 2 * k + 2].reshape(high, 2 * SUB, rank)
        finish(block, 2 * k)

    def owned_end(n, theirs):
        mine, other = direct + 2 * n, direct + owned + 2 * n
        target = 1 - side if theirs else side
        item = other if theirs else mine
        summed = dot(cur[top, mine : mine + 2].reshape(-1, rank), interp_ref[target, side])
        summed += dot(cur[top, other : other + 2].reshape(-1, rank), interp_ref[target, 1 - side])
        turned = rotate(
            summed.reshape(high, 2, SUB, rank),
            dcos[item : item + 2].reshape(high, SUB, rank),
            dsin[item : item + 2].reshape(high, SUB, rank),
        )
        block = turned.reshape(high, 2 * SUB, rank).astype(BF16)
        if not theirs:
            finish(block, item)
            return
        block = local_steps(block, item)
        for part in range(2):
            done[2 * n + part] = as_stored(block, part)
            copy_done(2 * n + part, side).start()

    tasks = []

    def task(when, work, *operands):
        tasks.append((when, len(tasks), work, operands))

    for item in range(items):
        theirs = item >= direct + owned
        begin = 3.8 + 2.8 * (item - direct - owned) if theirs else 0.1 * item
        task(begin, load, item)
        begin = begin + 0.8 if theirs else 1.0 + 0.3 * item
        task(begin, angles, item, 0, dcos, dsin)
        task(begin, device_step, 0, item)
        task(2.6 + 0.2 * item if item < direct else 3.0 + 1.4 * item, angles, item, 1, lcos, lsin)
        for level in range(1, top):
            when = 2.0 + 2.4 * level + 1.4 * item
            task(max(when, begin - 1.0 + 2.4 * level), device_step, level, item)
        if item < direct:
            task(2.6 + 2.4 * top + 2.8 * item, device_step, top, item)
    task(0.9, place, 0)
    task(0.95, fetch_interp.wait)
    task(3.5, place, 1)
    for k in range(nd):
        task(2.7 + 2.4 * top + 2.8 * (2 * k + 1), direct_end, k)
    for n in range(nf):
        last = direct + owned + 2 * n + 1
        when = 2.1 + 2.4 * (top - 1) + 1.4 * last
        when = max(when, 3.7 + 2.8 * (2 * n + 1) + 2.4 * (top - 1))
        task(when, owned_end, n, True)
        task(when + 3.0, owned_end, n, False)
    for _, _, work, operands in sorted(tasks, key=lambda entry: entry[:2]):
        work(*operands)

    for n in range(owned):
        copy_done(n, 1 - side).wait_recv()
        copy_raw(n).wait_send()
        copy_done(n, side).wait_send()
    copy_coord.wait_send()
    for level in range(depth):
        for item in range(items if level < top else direct):
            copy(level, item).wait_send()


def solution(mesh):
    levels = []
    for axis in ("bz", "by", "bx"):
        levels += [(axis, bit) for bit in range(mesh.shape[axis].bit_length() - 1)]

    def local(weights, interp, slowness, box_coord):
        per_dev, _, rank = weights.shape
        high = 1 << LOCAL
        nk = per_dev // (high * SUB)
        half = high // 2
        depth, chunks, rows = len(levels), 2 * nk, half * 2 * SUB
        stored = weights.reshape(per_dev, 2, 2, 128).transpose(0, 2, 1, 3)
        stored = stored.reshape(high, nk, 4 * SUB, 128)
        table = pltpu.VMEM((chunks, half, SUB, rank), F32)
        owned = nk // 4 * 2
        dma = pltpu.SemaphoreType.DMA
        result = pl.pallas_call(
            functools.partial(kernel, levels),
            out_shape=jax.ShapeDtypeStruct(stored.shape, BF16),
            in_specs=[pl.BlockSpec(memory_space=pltpu.HBM)] * 4,
            out_specs=pl.BlockSpec(memory_space=pltpu.VMEM),
            scratch_shapes=[
                pltpu.VMEM(stored.shape, BF16),
                pltpu.VMEM(interp.shape, BF16),
                pltpu.VMEM(slowness.shape, F32),
                pltpu.VMEM((2,) + box_coord.shape, jnp.int32),
                pltpu.VMEM((owned, half, 4 * SUB, 128), BF16),
                pltpu.VMEM((owned, half, 4 * SUB, 128), BF16),
                pltpu.VMEM((depth + 1, chunks, rows, rank), BF16),
                pltpu.VMEM((depth, chunks, rows, rank), BF16),
                table, table, table, table,
                pltpu.VMEM((8, per_dev), F32),
                pltpu.VMEM((2, high, nk, SUB, 8), F32),
                dma((nk + 3,)),
                dma((depth, chunks)), dma((depth, chunks)),
                dma((owned,)), dma((owned,)),
                dma, dma,
                dma((owned,)), dma((owned,)),
            ],
            compiler_params=pltpu.CompilerParams(
                collective_id=0, has_side_effects=True, vmem_limit_bytes=53 * 1024 * 1024
            ),
        )(stored, interp, slowness, box_coord)
        result = result.reshape(per_dev, 2, 2, 128).transpose(0, 2, 1, 3)
        return result.reshape(per_dev, 2, rank)

    return jax.shard_map(
        local,
        mesh=mesh,
        in_specs=(P(("shots", "bx", "by", "bz"), None, None), P(), P(), P(None, ("bx", "by", "bz"))),
        out_specs=P(("shots", "bx", "by", "bz"), None, None),
        check_vma=False,
    )
```

```python
import functools
import math

import jax
import jax.numpy as jnp
from jax import lax
from jax.experimental import pallas as pl
from jax.experimental.pallas import tpu as pltpu
from jax.sharding import PartitionSpec as P

LOCAL = 4
MESH = pl.DeviceIdType.MESH
F32 = jnp.float32
BF16 = jnp.bfloat16
SUB = 8

SIN_TERMS = [(-1) ** i * math.pi ** (2 * i + 1) / math.factorial(2 * i + 1) for i in range(6)]
COS_TERMS = [(-1) ** i * math.pi ** (2 * i) / math.factorial(2 * i) for i in range(6)]


def horner(terms, square):
    total = jnp.full_like(square, terms[-1])
    for term in terms[-2::-1]:
        total = total * square + term
    return total


def cos_sin(angle):
    turns = angle * (1.0 / (2.0 * math.pi))
    frac = turns - jnp.round(turns)
    square = frac * frac
    half_sin = frac * horner(SIN_TERMS, square)
    half_cos = horner(COS_TERMS, square)
    return 1.0 - 2.0 * half_sin * half_sin, 2.0 * half_sin * half_cos


def shuffle_matrix(rows, inverse):
    worked = lax.broadcasted_iota(jnp.int32, (rows, rows), 1 if inverse else 0)
    stored = lax.broadcasted_iota(jnp.int32, (rows, rows), 0 if inverse else 1)
    source = (
        (worked // 32) * 32
        + (worked % 8) * 4
        + ((worked // 16) % 2) * 2
        + (worked // 8) % 2
    )
    return jnp.where(stored == source, 1.0, 0.0).astype(BF16)


def rotate(summed, cosine, sine):
    real_part, imag_part = summed[:, 0], summed[:, 1]
    return jnp.stack(
        [cosine * real_part - sine * imag_part, sine * real_part + cosine * imag_part], axis=1
    )


def dot(a, b):
    return jnp.dot(a, b, preferred_element_type=F32)


def kernel(
    levels, w_hbm, interp_hbm, slow_hbm, coord_hbm, out_ref,
    w_ref, interp_ref, slow_ref, coord_ref, raw, done, cur, got,
    dcos, dsin, lcos, lsin, padded, columns,
    in_sem, send_sem, recv_sem, raw_send, raw_recv, coord_send, coord_recv, done_send, done_recv,
):
    depth = len(levels)
    top = depth - 1
    high, nk = w_ref.shape[0], w_ref.shape[1]
    half = high // 2
    rows = half * 2 * SUB
    rank = interp_ref.shape[-1]
    nd, nf = nk // 2, nk // 4
    direct, owned = 2 * nd, 2 * nf
    items = direct + 2 * owned

    upper, partner = [], []
    for axis, bit in levels:
        me = lax.axis_index(axis)
        up = (me // (1 << bit)) % 2
        upper.append(up)
        partner.append({axis: me + (1 << bit) * (1 - 2 * up)})
    side = upper[top]

    def group_of(item):
        if item < direct:
            return item // 2
        return nd + side * nf + ((item - direct) % owned) // 2

    def fetch(src, dst, n):
        return pltpu.make_async_copy(src, dst, in_sem.at[n])

    fetches = [
        fetch(w_hbm.at[:, group_of(2 * n)], w_ref.at[:, group_of(2 * n)], n) for n in range(nd + nf)
    ]
    fetch_coord = fetch(coord_hbm, coord_ref.at[0], nd + nf)
    fetch_slow = fetch(slow_hbm, slow_ref, nd + nf + 1)
    fetch_interp = fetch(interp_hbm, interp_ref, nd + nf + 2)
    for one in [fetches[0], fetch_coord, fetch_slow, fetch_interp] + fetches[1:]:
        one.start()

    barrier = pltpu.get_barrier_semaphore()
    for device in partner:
        pl.semaphore_signal(barrier, inc=1, device_id=device, device_id_type=MESH)
    pl.semaphore_wait(barrier, depth)

    def remote(src, dst, sent, received, level):
        return pltpu.make_async_remote_copy(
            src_ref=src, dst_ref=dst, send_sem=sent, recv_sem=received,
            device_id=partner[level], device_id_type=MESH,
        )

    def copy(level, item):
        return remote(
            cur.at[level, item], got.at[level, item],
            send_sem.at[level, item], recv_sem.at[level, item], level,
        )

    def copy_raw(n):
        group = nd + (1 - side) * nf + n // 2
        src = w_hbm.at[pl.ds((n % 2) * half, half), group]
        return remote(src, raw.at[n], raw_send.at[n], raw_recv.at[n], top)

    copy_coord = remote(coord_hbm, coord_ref.at[1], coord_send, coord_recv, top)

    def copy_done(n, owner):
        dst = out_ref.at[pl.ds((n % 2) * half, half), nd + owner * nf + n // 2]
        return remote(done.at[n], dst, done_send.at[n], done_recv.at[n], top)

    copy_coord.start()

    spread = shuffle_matrix(half * 32, False)
    gather = shuffle_matrix(half * 32, True)

    def load(item):
        if item < direct + owned:
            if item % 2 == 0:
                fetches[item // 2].wait()
            first = (item % 2) * half
            stored = w_ref[first : first + half, group_of(item)]
        else:
            n = item - direct - owned
            copy_raw(n).wait_recv()
            stored = raw[n]
        moved = dot(spread, stored.reshape(half * 32, 128)).reshape(half, 2, 2 * SUB, 128)
        block = jnp.concatenate([moved[:, 0], moved[:, 1]], axis=-1)
        cur[0, item] = block.reshape(rows, rank).astype(BF16)
        copy(0, item).start()

    def place(which):
        if which == 0:
            fetch_coord.wait()
            fetch_slow.wait()
            padded[...] = jnp.zeros_like(padded)
        else:
            copy_coord.wait_recv()
        padded[0:2] = coord_ref[which].astype(F32)
        columns[which] = padded[...].T.reshape(columns.shape[1:])

    def angles(item, table, cos_ref, sin_ref):
        first = (item % 2) * half
        which = 1 if item >= direct + owned else 0
        column = columns[which, first : first + half, group_of(item)].reshape(half * SUB, 8)
        angle = column[:, 0:1] * slow_ref[table, 0:1] + column[:, 1:2] * slow_ref[table, 1:2]
        cosine, sine = cos_sin(angle)
        cos_ref[item] = cosine.reshape(half, SUB, rank)
        sin_ref[item] = sine.reshape(half, SUB, rank)

    def device_step(level, item):
        up = upper[level]
        mine = dot(cur[level, item], interp_ref[up, up])
        copy(level, item).wait_recv()
        summed = mine + dot(got[level, item], interp_ref[up, 1 - up])
        turned = rotate(summed.reshape(half, 2, SUB, rank), dcos[item], dsin[item])
        cur[level + 1, item] = turned.reshape(rows, rank).astype(BF16)
        if level + 1 < top or (level + 1 == top and item < direct):
            copy(level + 1, item).start()

    def local_steps(block, item):
        cosine = lcos[item : item + 2].reshape(high, SUB, rank)
        sine = lsin[item : item + 2].reshape(high, SUB, rank)
        for num in range(LOCAL):
            outer, inner = 1 << num, high >> (num + 1)
            pair = block.reshape(outer, 2, inner, 2 * SUB, rank)
            first = pair[:, 0].reshape(-1, rank)
            second = pair[:, 1].reshape(-1, rank)
            cos_pair = cosine.reshape(outer, 2, inner, SUB, rank)
            sin_pair = sine.reshape(outer, 2, inner, SUB, rank)
            results = []
            for target in range(2):
                summed = dot(first, interp_ref[target, 0]) + dot(second, interp_ref[target, 1])
                turned = rotate(
                    summed.reshape(outer * inner, 2, SUB, rank),
                    cos_pair[:, target].reshape(-1, SUB, rank),
                    sin_pair[:, target].reshape(-1, SUB, rank),
                )
                results.append(turned.astype(BF16).reshape(outer, inner, 2 * SUB, rank))
            block = jnp.stack(results, axis=1).reshape(high, 2 * SUB, rank)
        return block

    def as_stored(block, part):
        piece = block[part * half : (part + 1) * half]
        worked = jnp.stack([piece[..., :128], piece[..., 128:]], axis=1)
        stored = dot(gather, worked.reshape(half * 32, 128))
        return stored.reshape(half, 32, 128).astype(BF16)

    def finish(block, item):
        block = local_steps(block, item)
        for part in range(2):
            out_ref[part * half : (part + 1) * half, group_of(item)] = as_stored(block, part)

    def direct_end(k):
        block = cur[depth, 2 * k : 2 * k + 2].reshape(high, 2 * SUB, rank)
        finish(block, 2 * k)

    def owned_end(n, theirs):
        mine, other = direct + 2 * n, direct + owned + 2 * n
        target = 1 - side if theirs else side
        item = other if theirs else mine
        summed = dot(cur[top, mine : mine + 2].reshape(-1, rank), interp_ref[target, side])
        summed += dot(cur[top, other : other + 2].reshape(-1, rank), interp_ref[target, 1 - side])
        turned = rotate(
            summed.reshape(high, 2, SUB, rank),
            dcos[item : item + 2].reshape(high, SUB, rank),
            dsin[item : item + 2].reshape(high, SUB, rank),
        )
        block = turned.reshape(high, 2 * SUB, rank).astype(BF16)
        if not theirs:
            finish(block, item)
            return
        block = local_steps(block, item)
        for part in range(2):
            done[2 * n + part] = as_stored(block, part)
            copy_done(2 * n + part, side).start()

    def start_raw(n):
        copy_raw(n).start()

    tasks = []

    def task(when, work, *operands):
        tasks.append((when, len(tasks), work, operands))

    for item in range(items):
        theirs = item >= direct + owned
        begin = 6.0 + 2.8 * (item - direct - owned) if theirs else 0.1 * item
        task(begin, load, item)
        begin = begin + 0.8 if theirs else 1.0 + 0.3 * item
        task(begin, angles, item, 0, dcos, dsin)
        task(begin, device_step, 0, item)
        task(2.6 + 0.2 * item if item < direct else 3.0 + 1.4 * item, angles, item, 1, lcos, lsin)
        for level in range(1, top):
            when = 2.0 + 2.4 * level + 1.4 * item
            task(max(when, begin - 1.0 + 2.4 * level), device_step, level, item)
        if item < direct:
            task(2.6 + 2.4 * top + 2.8 * item, device_step, top, item)
    for n in range(owned):
        task((-1.0, 5.0)[n % 2], start_raw, n)
    task(0.9, place, 0)
    task(0.95, fetch_interp.wait)
    task(3.5, place, 1)
    for k in range(nd):
        task(2.7 + 2.4 * top + 2.8 * (2 * k + 1), direct_end, k)
    for n in range(nf):
        last = direct + owned + 2 * n + 1
        when = 2.1 + 2.4 * (top - 1) + 1.4 * last
        when = max(when, 3.7 + 2.8 * (2 * n + 1) + 2.4 * (top - 1))
        task(when, owned_end, n, True)
        task(when + 3.0, owned_end, n, False)
    for _, _, work, operands in sorted(tasks, key=lambda entry: entry[:2]):
        work(*operands)

    for n in range(owned):
        copy_done(n, 1 - side).wait_recv()
        copy_raw(n).wait_send()
        copy_done(n, side).wait_send()
    copy_coord.wait_send()
    for level in range(depth):
        for item in range(items if level < top else direct):
            copy(level, item).wait_send()


def solution(mesh):
    levels = []
    for axis in ("bz", "by", "bx"):
        levels += [(axis, bit) for bit in range(mesh.shape[axis].bit_length() - 1)]

    def local(weights, interp, slowness, box_coord):
        per_dev, _, rank = weights.shape
        high = 1 << LOCAL
        nk = per_dev // (high * SUB)
        half = high // 2
        depth, chunks, rows = len(levels), 2 * nk, half * 2 * SUB
        stored = weights.reshape(per_dev, 2, 2, 128).transpose(0, 2, 1, 3)
        stored = stored.reshape(high, nk, 4 * SUB, 128)
        table = pltpu.VMEM((chunks, half, SUB, rank), F32)
        owned = nk // 4 * 2
        dma = pltpu.SemaphoreType.DMA
        result = pl.pallas_call(
            functools.partial(kernel, levels),
            out_shape=jax.ShapeDtypeStruct(stored.shape, BF16),
            in_specs=[pl.BlockSpec(memory_space=pltpu.HBM)] * 4,
            out_specs=pl.BlockSpec(memory_space=pltpu.VMEM),
            scratch_shapes=[
                pltpu.VMEM(stored.shape, BF16),
                pltpu.VMEM(interp.shape, BF16),
                pltpu.VMEM(slowness.shape, F32),
                pltpu.VMEM((2,) + box_coord.shape, jnp.int32),
                pltpu.VMEM((owned, half, 4 * SUB, 128), BF16),
                pltpu.VMEM((owned, half, 4 * SUB, 128), BF16),
                pltpu.VMEM((depth + 1, chunks, rows, rank), BF16),
                pltpu.VMEM((depth, chunks, rows, rank), BF16),
                table, table, table, table,
                pltpu.VMEM((8, per_dev), F32),
                pltpu.VMEM((2, high, nk, SUB, 8), F32),
                dma((nk + 3,)),
                dma((depth, chunks)), dma((depth, chunks)),
                dma((owned,)), dma((owned,)),
                dma, dma,
                dma((owned,)), dma((owned,)),
            ],
            compiler_params=pltpu.CompilerParams(
                collective_id=0, has_side_effects=True, vmem_limit_bytes=53 * 1024 * 1024
            ),
        )(stored, interp, slowness, box_coord)
        result = result.reshape(per_dev, 2, 2, 128).transpose(0, 2, 1, 3)
        return result.reshape(per_dev, 2, rank)

    return jax.shard_map(
        local,
        mesh=mesh,
        in_specs=(P(("shots", "bx", "by", "bz"), None, None), P(), P(), P(None, ("bx", "by", "bz"))),
        out_specs=P(("shots", "bx", "by", "bz"), None, None),
        check_vma=False,
    )
```
